32 devices in a mesh: ep: 8 (over z, x), tp: 4 (over y, core).
Axes of the slice: x: 2, y: 2, z: 4, core: 2. Of those that a mesh axis runs over, the one named last changes fastest.
Arguments:
- tokens: bfloat16 [2048, 3584], P('ep', 'tp'), may hold values from -6 to 6
- grad_out: bfloat16 [2048, 3584], P('ep', 'tp'), may hold values from -6 to 6
- route_ids: int32 [2048, 2], P('ep'), may hold values from 0 to 7, all different within a row; in each aligned block of 256 rows (0 to 255, 256 to 511, ...) at most 128 rows name the same one
- route_probs: float32 [2048, 2], P('ep'), may hold values from 0.2 to 1
- w_gate: bfloat16 [8, 3584, 1024], P('ep', None, 'tp'), may hold values from -0.09375 to 0.09375
- w_up: bfloat16 [8, 3584, 1024], P('ep', None, 'tp'), may hold values from -0.09375 to 0.09375
- w_down: bfloat16 [8, 1024, 3584], P('ep', 'tp'), may hold values from -0.1875 to 0.1875
Outputs:
- grad_tokens: bfloat16 [2048, 3584], P('ep', 'tp')
- grad_gate: bfloat16 [8, 3584, 1024], P('ep', None, 'tp')
- grad_up: bfloat16 [8, 3584, 1024], P('ep', None, 'tp')
- grad_down: bfloat16 [8, 1024, 3584], P('ep', 'tp')
The draws below stay inside these ranges and needn't reach their ends.
Inputs may be any that keep to these rules, and one draw needn't show every extreme that they name: `route_ids`: each token names 2 different experts. Among the tokens of one index of ep (aligned blocks of 256 tokens), no expert is named by more than 128 tokens, and in every draw some expert is named by exactly 128 of some block.
All inputs are finite; a program needn't handle non-finite values.
Results may differ from the reference program's by a relative error of at most 0.0065.
Values may be sent and summed in bfloat16 or wider, within the bound.
A program may use at most 128 MiB of HBM per device.

```python
import math
import jax
import jax.numpy as jnp
import numpy as np
from jax import lax

D = 3584
FF = 1024
TOP = 2
TOK_DEV = 256
TOKENS = 2048
EXPERTS = 8
CAP = 128
N_EP = 8


def shard_levels(rng, dims, pieces, low, high):
    def one(position, parts):
        heights = jax.random.uniform(jax.random.fold_in(jax.random.fold_in(rng, 6), position), (parts,), jnp.float32, low / len(pieces), high / len(pieces))
        return jnp.repeat(jnp.exp(heights), dims[position] // parts).reshape((-1,) + (1,) * (len(dims) - position - 1))

    gain = one(*pieces[0])
    for cut in pieces[1:]:
        gain = gain * one(*cut)
    return gain


def deal_out(key, own, number, rows, number_of, top, most, slope):
    sequence = jax.random.permutation(key, number_of)
    heavy_load, common = shares(number_of, rows * top, most, slope, True), shares(number_of, rows * top, most, slope, False)
    places = jnp.arange(number_of)

    def named(lengths, offset_by):
        used = int((lengths > 0).sum())
        fixed = max(1, used // 4)
        passed = fixed + (places - fixed + offset_by * (used - fixed)) % max(1, number_of - fixed)
        return jnp.zeros((number_of,), jnp.int32).at[sequence[jnp.where(places < fixed, places, passed)]].set(jnp.asarray(lengths, jnp.int32))

    lengths = jnp.where(number % 4 == 0, named(heavy_load, number // 4), named(common, number - number // 4 - 1))
    mixed = jax.random.permutation(jax.random.fold_in(own, 3), number_of)
    giver, sink = mixed[0:number_of // 2 * 2:2], mixed[1:number_of // 2 * 2:2]
    room = jnp.minimum(lengths[giver] - 1, most - lengths[sink]) // 2
    room = jnp.where((giver == sequence[0]) | (sink == sequence[0]) | (lengths[sink] == 0), 0, jnp.maximum(room, 0))
    passed = jax.random.randint(jax.random.fold_in(own, 4), (number_of // 2,), 0, 1 << 20) % (room + 1)
    lengths = lengths.at[giver].add(-passed).at[sink].add(passed)
    members = jnp.searchsorted(jnp.cumsum(lengths), jnp.arange(rows * top), side="right").astype(jnp.int32)
    listing = members.reshape(top, rows).T
    listing = listing[jax.random.permutation(jax.random.fold_in(own, 1), rows)]
    offset_by = jax.random.randint(jax.random.fold_in(own, 2), (rows, 1), 0, top)
    return jnp.take_along_axis(listing, (jnp.arange(top)[None, :] + offset_by) % top, axis=1)


def shares(count, total, bound, skew, full):
    weights = [(1 << 20) // math.isqrt(rank ** skew) + 1 for rank in range(1, count + 1)]
    largest = bound if full else min(bound, max(-(-total // count), total * weights[0] // sum(weights)))
    least = 1 if total - largest >= count - 1 else 0
    holding, rest = [largest] + [least] * (count - 1), total - largest - least * (count - 1)
    while rest > 0:
        movable = [i for i in range(1, count) if holding[i] < largest] or [i for i in range(1, count) if holding[i] < bound]
        mass, remaining = sum([weights[i] for i in movable]), rest
        for i in movable:
            addition = min(bound - holding[i], max(1, remaining * weights[i] // mass), rest)
            holding[i] = holding[i] + addition
            rest = rest - addition
    return np.array(holding)


def bell_draw(key, extent, spread, bound, split=(), kind=jnp.bfloat16):
    result = spread * jax.random.normal(key, extent, jnp.float32)
    if split:
        result = result * shard_levels(key, extent, split, -0.22, 0.18)
    return jnp.clip(result, -bound, bound).astype(kind)


def setup_inputs(seed: int = 0) -> dict:
    key_of = jax.random.split(jax.random.key(seed), 8)
    tokens = bell_draw(key_of[0], (TOKENS, D), 1.0, 6.0, ((0, 8), (1, 4)))
    grad_out = bell_draw(key_of[1], (TOKENS, D), 1.0, 6.0, ((0, 8), (1, 4)))
    route_ids_keys = jax.random.split(jax.random.fold_in(key_of[2], 1), TOKENS // TOK_DEV)
    route_ids_turns = jax.random.permutation(jax.random.fold_in(key_of[2], 3), TOKENS // TOK_DEV)
    route_ids = jax.vmap(lambda own, number: deal_out(jax.random.fold_in(key_of[2], 2), own, number, TOK_DEV, EXPERTS, TOP, CAP, 1))(route_ids_keys, route_ids_turns).reshape((TOKENS, TOP))
    route_probs = jnp.clip(0.2 + 0.8 * jax.random.uniform(key_of[3], (TOKENS, TOP), jnp.float32) ** shard_levels(key_of[3], (TOKENS, TOP), ((0, 8),), -0.2, 0.2), 0.2, 1.0)
    w_gate = bell_draw(key_of[4], (EXPERTS, D, FF), D ** -0.5, 0.09375, ((0, 8), (2, 4)))
    w_up = bell_draw(key_of[5], (EXPERTS, D, FF), D ** -0.5, 0.09375, ((0, 8), (2, 4)))
    w_down = bell_draw(key_of[6], (EXPERTS, FF, D), FF ** -0.5, 0.1875, ((0, 8), (1, 4)))
    return {"tokens": tokens, "grad_out": grad_out, "route_ids": route_ids, "route_probs": route_probs, "w_gate": w_gate, "w_up": w_up, "w_down": w_down}


def contract_last(left, right):
    return lax.dot_general(left, right, (((1,), (1,)), ((), ())), preferred_element_type=jnp.float32)


def contract_first(left, right):
    return lax.dot_general(left, right, (((0,), (0,)), ((), ())), preferred_element_type=jnp.float32)


def row_pass(x_rows, s_rows, gate_cols, up_cols, down_rows):
    gate = jnp.dot(x_rows, gate_cols, preferred_element_type=jnp.float32)
    upper = jnp.dot(x_rows, up_cols, preferred_element_type=jnp.float32)
    sigma = jax.nn.sigmoid(gate)
    active = gate * sigma
    hidden = (active * upper).astype(jnp.bfloat16)
    back = contract_last(s_rows, down_rows)
    d_up = (back * active).astype(jnp.bfloat16)
    d_gate = (back * upper * sigma * (1.0 + gate * (1.0 - sigma))).astype(jnp.bfloat16)
    return d_gate, d_up, contract_first(x_rows, d_gate), contract_first(x_rows, d_up), contract_first(hidden, s_rows)


def reference(tokens, grad_out, route_ids, route_probs, w_gate, w_up, w_down):
    routes = TOKENS * TOP
    rows_e = N_EP * CAP
    flat_ids = route_ids.reshape(-1).astype(jnp.int32)
    onehot = (flat_ids[:, None] == jnp.arange(EXPERTS, dtype=jnp.int32)[None, :]).astype(jnp.int32)
    rank = jnp.sum((jnp.cumsum(onehot, axis=0) - onehot) * onehot, axis=1).astype(jnp.int32)
    table = jnp.full((EXPERTS * rows_e,), routes, dtype=jnp.int32)
    table = table.at[flat_ids * rows_e + rank].set(jnp.arange(routes, dtype=jnp.int32))
    flat_probs = route_probs.reshape(-1)

    def per_expert(total, expert):
        index = lax.dynamic_slice_in_dim(table, expert * rows_e, rows_e)
        live = index < routes
        token = jnp.where(live, index // TOP, TOKENS).astype(jnp.int32)
        x_rows = jnp.take(tokens, token, axis=0, mode="fill", fill_value=0)
        prob = jnp.where(live, jnp.take(flat_probs, jnp.where(live, index, 0).astype(jnp.int32)), 0.0)
        dy_rows = jnp.take(grad_out, token, axis=0, mode="fill", fill_value=0).astype(jnp.float32)
        s_rows = (prob[:, None] * dy_rows).astype(jnp.bfloat16)
        d_gate, d_up, g_gate, g_up, g_down = row_pass(x_rows, s_rows, w_gate[expert], w_up[expert], w_down[expert])
        route_dx = (contract_last(d_gate, w_gate[expert]) + contract_last(d_up, w_up[expert])).astype(jnp.bfloat16)
        total = total.at[token].add(route_dx.astype(jnp.float32), mode="drop")
        return total, (g_gate.astype(jnp.bfloat16), g_up.astype(jnp.bfloat16), g_down.astype(jnp.bfloat16))

    total, grads = lax.scan(per_expert, jnp.zeros((TOKENS, D), jnp.float32), jnp.arange(EXPERTS, dtype=jnp.int32))
    return total.astype(jnp.bfloat16), grads[0], grads[1], grads[2]
```

```python
import functools

import jax
import jax.numpy as jnp
from jax import lax
from jax.experimental import pallas as pl
from jax.experimental.pallas import tpu as pltpu
from jax.sharding import PartitionSpec as P

F32 = jnp.float32
BF16 = jnp.bfloat16


def mul(left, right):
    return jnp.dot(left, right, preferred_element_type=F32)


def contract_last(left, right):
    return lax.dot_general(left, right, (((1,), (1,)), ((), ())), preferred_element_type=F32)


def contract_first(left, right):
    return lax.dot_general(left, right, (((0,), (0,)), ((), ())), preferred_element_type=F32)


def kernel(
    n, tok, gout, code, prob, wg, wu, wd,
    g_tok, g_gate, g_up, g_down,
    stage, xs, dg, du, hid, dxp, dxr, dyr, back, acc,
    ep_s, ep_r, ya_s, ya_r, ma_s, ma_r, mb_s, mb_r, dm_s, dm_r, dy_s, dy_r, rt_s, rt_r,
):
    me = lax.axis_index("ep")
    t = lax.axis_index("tp")
    low = lax.rem(t, 2)
    high = t // 2
    mate = t + 1 - 2 * low
    across = lax.rem(t + 2, 4)
    cap, quarter = stage.shape[2], stage.shape[3]
    rows = tok.shape[0]

    barrier = pltpu.get_barrier_semaphore()

    def greet(j, carry):
        pl.semaphore_signal(barrier, inc=1, device_id={"ep": lax.rem(me + j, n)})
        return carry

    lax.fori_loop(1, n, greet, 0)
    pl.semaphore_signal(barrier, inc=1, device_id={"tp": mate})
    pl.semaphore_signal(barrier, inc=1, device_id={"tp": across})
    pl.semaphore_wait(barrier, n + 1)

    def copy(src, dst, send, recv, j, to):
        return pltpu.make_async_remote_copy(
            src_ref=src, dst_ref=dst, send_sem=send.at[j], recv_sem=recv.at[j], device_id=to
        )

    def ep_copy(j):
        return copy(stage.at[j], xs.at[j, t], ep_s, ep_r, j, {"ep": lax.rem(me + j, n)})

    def across_copy(j):
        return copy(xs.at[j, t], xs.at[j, t], ya_s, ya_r, j, {"tp": across})

    def mate_copy(j):
        return copy(xs.at[j, t], xs.at[j, t], ma_s, ma_r, j, {"tp": mate})

    def relay_copy(j):
        return copy(xs.at[j, across], xs.at[j, across], mb_s, mb_r, j, {"tp": mate})

    def part_copy(j):
        return copy(dxp.at[j, 1 - low], dxr.at[j], dm_s, dm_r, j, {"tp": mate})

    def half_copy(j):
        return copy(dxp.at[j, low, 1 - high], dyr.at[j], dy_s, dy_r, j, {"tp": across})

    def return_copy(j):
        return copy(
            dxp.at[j, low, high], back.at[j], rt_s, rt_r, j, {"ep": lax.rem(me - j + n, n)}
        )

    def chosen(j):
        expert = lax.rem(me + j, n)
        return lax.broadcasted_iota(jnp.int32, (cap, rows), 0) == code[expert]

    def pack(j):
        pick = chosen(j)
        share = jnp.sum(jnp.where(pick, prob[lax.rem(me + j, n)], 0.0), axis=1, keepdims=True)
        onehot = pick.astype(F32).astype(BF16)
        return mul(onehot, tok[...]).astype(BF16), (share * mul(onehot, gout[...])).astype(BF16)

    def send(j, carry):
        x_rows, s_rows = pack(j)
        stage[j, 0] = x_rows
        stage[j, 1] = s_rows
        ep_copy(j).start()
        return carry

    lax.fori_loop(1, n, send, 0)
    x_rows, s_rows = pack(0)
    xs[0, t, 0] = x_rows
    xs[0, t, 1] = s_rows

    def compute(j):
        gate = jnp.zeros((cap, wg.shape[1]), F32)
        upper, down = gate, gate
        for q in range(4):
            at = slice(q * quarter, (q + 1) * quarter)
            x = xs[j, q, 0]
            gate += mul(x, wg[at, :])
            upper += mul(x, wu[at, :])
            down += contract_last(xs[j, q, 1], wd[:, at])
        sigma = jax.nn.sigmoid(gate)
        active = gate * sigma
        hid[j] = (active * upper).astype(BF16)
        d_up = (down * active).astype(BF16)
        d_gate = (down * upper * sigma * (1.0 + gate * (1.0 - sigma))).astype(BF16)
        dg[j] = d_gate
        du[j] = d_up
        for q in range(4):
            at = slice(q * quarter, (q + 1) * quarter)
            part = contract_last(d_gate, wg[at, :]) + contract_last(d_up, wu[at, :])
            dxp[j, q % 2, q // 2] = part.astype(BF16)

    def step(i, carry):
        @pl.when(i < n)
        def _():
            @pl.when(i > 0)
            def _():
                ep_copy(i).wait_recv()

            across_copy(i).start()
            mate_copy(i).start()

        @pl.when(jnp.logical_and(i >= 1, i < n + 1))
        def _():
            j = i - 1
            across_copy(j).wait_recv()
            relay_copy(j).start()

        @pl.when(jnp.logical_and(i >= 2, i < n + 2))
        def _():
            j = i - 2
            mate_copy(j).wait_recv()
            relay_copy(j).wait_recv()
            compute(j)
            part_copy(j).start()

        @pl.when(jnp.logical_and(i >= 3, i < n + 3))
        def _():
            j = i - 3
            part_copy(j).wait_recv()
            for h in range(2):
                dxp[j, low, h] = (dxp[j, low, h].astype(F32) + dxr[j, h].astype(F32)).astype(BF16)
            half_copy(j).start()

        @pl.when(i >= 4)
        def _():
            j = i - 4
            half_copy(j).wait_recv()
            total = (dxp[j, low, high].astype(F32) + dyr[j].astype(F32)).astype(BF16)

            @pl.when(j == 0)
            def _():
                back[0] = total

            @pl.when(j > 0)
            def _():
                dxp[j, low, high] = total
                return_copy(j).start()

        return carry

    lax.fori_loop(0, n + 4, step, 0)

    def grads(q, carry):
        at = pl.ds(pl.multiple_of(q * quarter, 128), quarter)
        x = xs[:, q, 0].reshape(n * cap, quarter)
        g_gate[at, :] = contract_first(x, dg[...].reshape(n * cap, -1)).astype(BF16)
        g_up[at, :] = contract_first(x, du[...].reshape(n * cap, -1)).astype(BF16)
        s = xs[:, q, 1].reshape(n * cap, quarter)
        g_down[:, at] = contract_first(hid[...].reshape(n * cap, -1), s).astype(BF16)
        return carry

    lax.fori_loop(0, 4, grads, 0)

    acc[...] = contract_first(chosen(0).astype(F32).astype(BF16), back[0])

    def gather(j, carry):
        return_copy(j).wait_recv()
        acc[...] += contract_first(chosen(j).astype(F32).astype(BF16), back[j])
        return carry

    lax.fori_loop(1, n, gather, 0)
    g_tok[...] = acc[...].astype(BF16)

    def drain(j, carry):
        @pl.when(j > 0)
        def _():
            ep_copy(j).wait_send()
            return_copy(j).wait_send()

        across_copy(j).wait_send()
        mate_copy(j).wait_send()
        relay_copy(j).wait_send()
        part_copy(j).wait_send()
        half_copy(j).wait_send()
        return carry

    lax.fori_loop(0, n, drain, 0)


def per_device(tokens, grad_out, route_ids, route_probs, w_gate, w_up, w_down):
    n = lax.axis_size("ep")
    tp = lax.axis_size("tp")
    rows, quarter = tokens.shape
    top = route_ids.shape[1]
    width, ff = w_gate.shape[1:]
    cap = max(2, 2 * rows * top // n)
    experts = jnp.arange(n, dtype=jnp.int32)[:, None]
    named = [route_ids[:, k][None, :] == experts for k in range(top)]
    prob = sum(jnp.where(named[k], route_probs[:, k][None, :], 0.0) for k in range(top))
    mask = functools.reduce(jnp.logical_or, named)
    earlier = jnp.arange(rows)[:, None] < jnp.arange(rows)[None, :]
    rank = mul(mask.astype(BF16), earlier.astype(BF16)).astype(jnp.int32)
    code = jnp.where(mask, rank, -1)
    sems = pltpu.SemaphoreType.DMA((n,))
    vmem = pl.BlockSpec(memory_space=pltpu.VMEM)
    g_tok, g_gate, g_up, g_down = pl.pallas_call(
        functools.partial(kernel, n),
        out_shape=(
            jax.ShapeDtypeStruct((rows, quarter), BF16),
            jax.ShapeDtypeStruct((width, ff), BF16),
            jax.ShapeDtypeStruct((width, ff), BF16),
            jax.ShapeDtypeStruct((ff, width), BF16),
        ),
        in_specs=[vmem] * 7,
        out_specs=(vmem,) * 4,
        scratch_shapes=[
            pltpu.VMEM((n, 2, cap, quarter), BF16),
            pltpu.VMEM((n, tp, 2, cap, quarter), BF16),
            pltpu.VMEM((n, cap, ff), BF16),
            pltpu.VMEM((n, cap, ff), BF16),
            pltpu.VMEM((n, cap, ff), BF16),
            pltpu.VMEM((n, 2, 2, cap, quarter), BF16),
            pltpu.VMEM((n, 2, cap, quarter), BF16),
            pltpu.VMEM((n, cap, quarter), BF16),
            pltpu.VMEM((n, cap, quarter), BF16),
            pltpu.VMEM((rows, quarter), F32),
        ]
        + [sems] * 14,
        compiler_params=pltpu.CompilerParams(
            collective_id=0, has_side_effects=True, vmem_limit_bytes=60 * 1024 * 1024
        ),
    )(
        tokens, grad_out, code.reshape(n, 1, rows), prob.reshape(n, 1, rows),
        w_gate[0], w_up[0], w_down[0],
    )
    return g_tok, g_gate[None], g_up[None], g_down[None]


def solution(mesh):
    placed = (
        P("ep", "tp"),
        P("ep", "tp"),
        P("ep", None),
        P("ep", None),
        P("ep", None, "tp"),
        P("ep", None, "tp"),
        P("ep", "tp", None),
    )
    return jax.shard_map(
        per_device,
        mesh=mesh,
        in_specs=placed,
        out_specs=(P("ep", "tp"), P("ep", None, "tp"), P("ep", None, "tp"), P("ep", "tp", None)),
        check_vma=False,
    )
```

```python
import functools

import jax
import jax.numpy as jnp
from jax import lax
from jax.experimental import pallas as pl
from jax.experimental.pallas import tpu as pltpu
from jax.sharding import PartitionSpec as P

F32 = jnp.float32
BF16 = jnp.bfloat16


def mul(left, right):
    return jnp.dot(left, right, preferred_element_type=F32)


def contract_last(left, right):
    return lax.dot_general(left, right, (((1,), (1,)), ((), ())), preferred_element_type=F32)


def contract_first(left, right):
    return lax.dot_general(left, right, (((0,), (0,)), ((), ())), preferred_element_type=F32)


def kernel(
    n, tok, gout, code, prob, wg, wu, wd,
    g_tok, g_gate, g_up, g_down,
    stage, xs, dg, du, hid, dxp, dxr, dyr, back, acc,
    ep_s, ep_r, ya_s, ya_r, ma_s, ma_r, mb_s, mb_r, dm_s, dm_r, dy_s, dy_r, rt_s, rt_r,
):
    me = lax.axis_index("ep")
    t = lax.axis_index("tp")
    low = lax.rem(t, 2)
    high = t // 2
    mate = t + 1 - 2 * low
    across = lax.rem(t + 2, 4)
    cap, quarter = stage.shape[2], stage.shape[3]
    rows = tok.shape[0]

    barrier = pltpu.get_barrier_semaphore()

    def greet(j, carry):
        pl.semaphore_signal(barrier, inc=1, device_id={"ep": lax.rem(me + j, n)})
        return carry

    lax.fori_loop(1, n, greet, 0)
    pl.semaphore_signal(barrier, inc=1, device_id={"tp": mate})
    pl.semaphore_signal(barrier, inc=1, device_id={"tp": across})
    pl.semaphore_wait(barrier, n + 1)

    def copy(src, dst, send, recv, j, to):
        return pltpu.make_async_remote_copy(
            src_ref=src, dst_ref=dst, send_sem=send.at[j], recv_sem=recv.at[j], device_id=to
        )

    def ep_copy(j):
        return copy(stage.at[j], xs.at[j, t], ep_s, ep_r, j, {"ep": lax.rem(me + j, n)})

    def across_copy(j):
        return copy(xs.at[j, t], xs.at[j, t], ya_s, ya_r, j, {"tp": across})

    def mate_copy(j):
        return copy(xs.at[j, t], xs.at[j, t], ma_s, ma_r, j, {"tp": mate})

    def relay_copy(j):
        return copy(xs.at[j, across], xs.at[j, across], mb_s, mb_r, j, {"tp": mate})

    def part_copy(j):
        return copy(dxp.at[j, 1 - low], dxr.at[j], dm_s, dm_r, j, {"tp": mate})

    def half_copy(j):
        return copy(dxp.at[j, low, 1 - high], dyr.at[j], dy_s, dy_r, j, {"tp": across})

    def return_copy(j):
        return copy(
            dxp.at[j, low, high], back.at[j], rt_s, rt_r, j, {"ep": lax.rem(me - j + n, n)}
        )

    def near(k):
        odd = lax.rem(k, 2)
        return odd * lax.div(k + 1, 2) + (1 - odd) * lax.rem(n - lax.div(k, 2), n)

    def chosen(j):
        expert = lax.rem(me + j, n)
        return lax.broadcasted_iota(jnp.int32, (cap, rows), 0) == code[expert]

    def pack(j):
        pick = chosen(j)
        share = jnp.sum(jnp.where(pick, prob[lax.rem(me + j, n)], 0.0), axis=1, keepdims=True)
        onehot = pick.astype(F32).astype(BF16)
        return mul(onehot, tok[...]).astype(BF16), (share * mul(onehot, gout[...])).astype(BF16)

    def send(k, carry):
        j = near(k)
        x_rows, s_rows = pack(j)
        stage[j, 0] = x_rows
        stage[j, 1] = s_rows
        ep_copy(j).start()
        return carry

    lax.fori_loop(1, n, send, 0)
    x_rows, s_rows = pack(0)
    xs[0, t, 0] = x_rows
    xs[0, t, 1] = s_rows

    def compute(j):
        gate = jnp.zeros((cap, wg.shape[1]), F32)
        upper, down = gate, gate
        for q in range(4):
            at = slice(q * quarter, (q + 1) * quarter)
            x = xs[j, q, 0]
            gate += mul(x, wg[at, :])
            upper += mul(x, wu[at, :])
            down += contract_last(xs[j, q, 1], wd[:, at])
        sigma = jax.nn.sigmoid(gate)
        active = gate * sigma
        hid[j] = (active * upper).astype(BF16)
        d_up = (down * active).astype(BF16)
        d_gate = (down * upper * sigma * (1.0 + gate * (1.0 - sigma))).astype(BF16)
        dg[j] = d_gate
        du[j] = d_up
        for q in range(4):
            at = slice(q * quarter, (q + 1) * quarter)
            part = contract_last(d_gate, wg[at, :]) + contract_last(d_up, wu[at, :])
            dxp[j, q % 2, q // 2] = part.astype(BF16)

    def grads(q):
        at = pl.ds(pl.multiple_of(q * quarter, 128), quarter)
        x = xs[:, q, 0].reshape(n * cap, quarter)
        g_gate[at, :] = contract_first(x, dg[...].reshape(n * cap, -1)).astype(BF16)
        g_up[at, :] = contract_first(x, du[...].reshape(n * cap, -1)).astype(BF16)
        s = xs[:, q, 1].reshape(n * cap, quarter)
        g_down[:, at] = contract_first(hid[...].reshape(n * cap, -1), s).astype(BF16)

    def step(i, carry):
        @pl.when(i >= 4)
        def _():
            j = near(i - 4)
            half_copy(j).wait_recv()
            total = (dxp[j, low, high].astype(F32) + dyr[j].astype(F32)).astype(BF16)

            @pl.when(j == 0)
            def _():
                back[0] = total

            @pl.when(j > 0)
            def _():
                dxp[j, low, high] = total
                return_copy(j).start()

        @pl.when(jnp.logical_and(i >= 3, i < n + 3))
        def _():
            j = near(i - 3)
            part_copy(j).wait_recv()
            for h in range(2):
                dxp[j, low, h] = (dxp[j, low, h].astype(F32) + dxr[j, h].astype(F32)).astype(BF16)
            half_copy(j).start()

        @pl.when(jnp.logical_and(i >= 2, i < n + 2))
        def _():
            j = near(i - 2)
            mate_copy(j).wait_recv()
            relay_copy(j).wait_recv()
            compute(j)
            part_copy(j).start()

        @pl.when(jnp.logical_and(i >= 1, i < n + 1))
        def _():
            j = near(i - 1)
            across_copy(j).wait_recv()
            relay_copy(j).start()

        @pl.when(i < n)
        def _():
            @pl.when(i > 0)
            def _():
                ep_copy(near(i)).wait_recv()

            across_copy(near(i)).start()
            mate_copy(near(i)).start()

        @pl.when(i >= n + 2)
        def _():
            grads(i - n - 2)

        return carry

    lax.fori_loop(0, n + 4, step, 0)

    def rest(q, carry):
        grads(q)
        return carry

    lax.fori_loop(2, 4, rest, 0)

    acc[...] = contract_first(chosen(0).astype(F32).astype(BF16), back[0])

    def gather(j, carry):
        return_copy(j).wait_recv()
        acc[...] += contract_first(chosen(j).astype(F32).astype(BF16), back[j])
        return carry

    lax.fori_loop(1, n, gather, 0)
    g_tok[...] = acc[...].astype(BF16)

    def drain(j, carry):
        @pl.when(j > 0)
        def _():
            ep_copy(j).wait_send()
            return_copy(j).wait_send()

        across_copy(j).wait_send()
        mate_copy(j).wait_send()
        relay_copy(j).wait_send()
        part_copy(j).wait_send()
        half_copy(j).wait_send()
        return carry

    lax.fori_loop(0, n, drain, 0)


def per_device(tokens, grad_out, route_ids, route_probs, w_gate, w_up, w_down):
    n = lax.axis_size("ep")
    tp = lax.axis_size("tp")
    rows, quarter = tokens.shape
    top = route_ids.shape[1]
    width, ff = w_gate.shape[1:]
    cap = max(2, 2 * rows * top // n)
    experts = jnp.arange(n, dtype=jnp.int32)[:, None]
    named = [route_ids[:, k][None, :] == experts for k in range(top)]
    prob = sum(jnp.where(named[k], route_probs[:, k][None, :], 0.0) for k in range(top))
    mask = functools.reduce(jnp.logical_or, named)
    earlier = jnp.arange(rows)[:, None] < jnp.arange(rows)[None, :]
    rank = mul(mask.astype(BF16), earlier.astype(BF16)).astype(jnp.int32)
    code = jnp.where(mask, rank, -1)
    sems = pltpu.SemaphoreType.DMA((n,))
    vmem = pl.BlockSpec(memory_space=pltpu.VMEM)
    g_tok, g_gate, g_up, g_down = pl.pallas_call(
        functools.partial(kernel, n),
        out_shape=(
            jax.ShapeDtypeStruct((rows, quarter), BF16),
            jax.ShapeDtypeStruct((width, ff), BF16),
            jax.ShapeDtypeStruct((width, ff), BF16),
            jax.ShapeDtypeStruct((ff, width), BF16),
        ),
        in_specs=[vmem] * 7,
        out_specs=(vmem,) * 4,
        scratch_shapes=[
            pltpu.VMEM((n, 2, cap, quarter), BF16),
            pltpu.VMEM((n, tp, 2, cap, quarter), BF16),
            pltpu.VMEM((n, cap, ff), BF16),
            pltpu.VMEM((n, cap, ff), BF16),
            pltpu.VMEM((n, cap, ff), BF16),
            pltpu.VMEM((n, 2, 2, cap, quarter), BF16),
            pltpu.VMEM((n, 2, cap, quarter), BF16),
            pltpu.VMEM((n, cap, quarter), BF16),
            pltpu.VMEM((n, cap, quarter), BF16),
            pltpu.VMEM((rows, quarter), F32),
        ]
        + [sems] * 14,
        compiler_params=pltpu.CompilerParams(
            collective_id=0, has_side_effects=True, vmem_limit_bytes=60 * 1024 * 1024
        ),
    )(
        tokens, grad_out, code.reshape(n, 1, rows), prob.reshape(n, 1, rows),
        w_gate[0], w_up[0], w_down[0],
    )
    return g_tok, g_gate[None], g_up[None], g_down[None]


def solution(mesh):
    placed = (
        P("ep", "tp"),
        P("ep", "tp"),
        P("ep", None),
        P("ep", None),
        P("ep", None, "tp"),
        P("ep", None, "tp"),
        P("ep", "tp", None),
    )
    return jax.shard_map(
        per_device,
        mesh=mesh,
        in_specs=placed,
        out_specs=(P("ep", "tp"), P("ep", None, "tp"), P("ep", None, "tp"), P("ep", "tp", None)),
        check_vma=False,
    )
```
